256 devices in a mesh: row: 32 (over x_hi, z, core), col: 8 (over x_lo, y).
Axes of the slice: x: 4 (x_hi: 2, x_lo: 2; x = x_hi * 2 + x_lo), y: 4, z: 8, core: 2. Of those that a mesh axis runs over, the one named last changes fastest.
Arguments:
- rates: bfloat16 [32768, 32896], P('row', 'col'), may hold values from -0.03125 to 0.03125
- trial: bfloat16 [32896, 512], P('col', 'row'), may hold values from -6 to 6
- test: bfloat16 [32768, 512], P('row', 'col'), may hold values from -0.03125 to 0.03125
- col_energy: float32 [32896], P('col'), may hold values from 0 to 4
- row_energy: float32 [32768], P('row'), may hold values from 0 to 4
Outputs:
- reduced: float32 [512, 512], P('col', 'row')
The draws below stay inside these ranges and needn't reach their ends.
All inputs are finite; a program needn't handle non-finite values.
Results may differ from the reference program's by a relative error of at most 0.0065.
Values may be sent and summed in bfloat16 or wider, within the bound.
No kernel may reach another device: no remote copies, remote signals or barrier semaphores. Data moves between devices by JAX's collectives and lax.ppermute only.
A program may use at most 64 MiB of HBM per device.

```python
import jax
import jax.numpy as jnp
from jax import lax

M = 32896
R = 512
ROWS_DEV = 1024
ROWS = 32768
N_ROW = 32


def block_scale(key, shape, shards, low, top_value):
    def one(dim, parts):
        heights = jax.random.uniform(jax.random.fold_in(jax.random.fold_in(key, 6), dim), (parts,), jnp.float32, low / len(shards), top_value / len(shards))
        return jnp.repeat(jnp.exp(heights), shape[dim] // parts).reshape((-1,) + (1,) * (len(shape) - dim - 1))

    loudness = one(*shards[0])
    for cut in shards[1:]:
        loudness = loudness * one(*cut)
    return loudness


def gaussian(stream_key, shape, scale, limit, pieces=(), held_as=jnp.bfloat16):
    values = scale * jax.random.normal(stream_key, shape, jnp.float32)
    if pieces:
        values = values * block_scale(stream_key, shape, pieces, -0.22, 0.18)
    return jnp.clip(values, -limit, limit).astype(held_as)


def setup_inputs(seed: int = 0) -> dict:
    seeds = jax.random.split(jax.random.key(seed), 6)
    rates = gaussian(seeds[0], (ROWS, M), M ** -0.5, 0.03125, ((0, 32), (1, 8)))
    trial = gaussian(seeds[1], (M, R), 1.0, 6.0, ((0, 8), (1, 32)))
    test = gaussian(seeds[2], (ROWS, R), ROWS ** -0.5, 0.03125, ((0, 32), (1, 8)))
    col_energy = jnp.clip(4.0 * jax.random.uniform(seeds[3], (M,), jnp.float32) ** block_scale(seeds[3], (M,), ((0, 8),), -0.2, 0.2), 0.0, 4.0)
    row_energy = jnp.clip(4.0 * jax.random.uniform(seeds[4], (ROWS,), jnp.float32) ** block_scale(seeds[4], (ROWS,), ((0, 32),), -0.2, 0.2), 0.0, 4.0)
    return {"rates": rates, "trial": trial, "test": test, "col_energy": col_energy, "row_energy": row_energy}


def reference(rates, trial, test, col_energy, row_energy):
    scaled_trial = (trial.astype(jnp.float32) * jnp.exp(-0.5 * col_energy)[:, None]).astype(jnp.bfloat16)
    scaled_wide = scaled_trial.astype(jnp.float32)
    blocks = rates.reshape(N_ROW, ROWS_DEV, M)

    def one_block(block):
        return jnp.dot(block.astype(jnp.float32), scaled_wide, precision=lax.Precision.HIGHEST)

    product = lax.map(one_block, blocks).reshape(ROWS, R)
    weighted_test = (test.astype(jnp.float32) * jnp.exp(0.5 * row_energy)[:, None]).astype(jnp.bfloat16)
    return jnp.dot(weighted_test.astype(jnp.float32).T, product, precision=lax.Precision.HIGHEST)
```

```python
import functools

import jax
import jax.numpy as jnp
from jax import lax
from jax.experimental import pallas as pl
from jax.experimental.pallas import tpu as pltpu
from jax.sharding import Mesh
from jax.sharding import PartitionSpec as P

SIZES = {"xh": 2, "z": 8, "core": 2, "xl": 2, "y": 4}
ROW, COL = ("xh", "z", "core"), ("xl", "y")
PEERS = ("xh", "z", "xl", "y")
F32, BF16 = jnp.float32, jnp.bfloat16
NT = (((1,), (1,)), ((), ()))


def shift(value, axis, by):
    n = SIZES[axis]
    return lax.ppermute(value, axis, [(i, (i + by) % n) for i in range(n)])


def project_kernel(place, *refs):
    blocks, energy, weight, own, other, out, basis, total = refs[:16], *refs[16:]
    step, steps = pl.program_id(0), pl.num_programs(0)

    @pl.when(step == 0)
    def _():
        scale = jnp.exp(-0.5 * energy[...])
        for n, block in enumerate(blocks):
            rows = pl.ds(pl.multiple_of(place[n] * 16, 16), 16)
            basis[rows, :] = (block[...].astype(F32) * scale).astype(BF16)
        total[...] = jnp.zeros_like(total)

    def add(rates):
        product = jnp.dot(basis[...], rates[...], preferred_element_type=F32).astype(BF16)
        total[...] += lax.dot_general(product, weight[...], NT, preferred_element_type=F32)

    @pl.when(step < steps // 2)
    def _():
        add(own)

    @pl.when(step >= steps // 2)
    def _():
        add(other)

    @pl.when(step == steps - 1)
    def _():
        left = lax.broadcasted_iota(jnp.int32, (8, 128), 1) < 64
        for j in range(16):
            for i in range(4):
                low = total[16 * j : 16 * j + 8, 128 * i : 128 * i + 128]
                high = total[16 * j + 8 : 16 * j + 16, 128 * i : 128 * i + 128]
                first = jnp.where(left, low, pltpu.roll(high, 64, 1))
                second = jnp.where(left, pltpu.roll(low, 64, 1), high)
                pair = jnp.concatenate([first, second], axis=0)
                out[64 * j + 16 * i : 64 * j + 16 * i + 16, :] = pair.astype(BF16)


def project(place, blocks, energy, weight, own, other):
    depth, rows = own.shape
    tile = 256
    half = rows // tile
    whole = lambda shape: pl.BlockSpec(shape, lambda s, p: (0, 0))
    return pl.pallas_call(
        project_kernel,
        grid_spec=pltpu.PrefetchScalarGridSpec(
            num_scalar_prefetch=1,
            grid=(2 * half,),
            in_specs=[whole((16, depth))] * 16
            + [
                whole((1, depth)),
                pl.BlockSpec((512, tile), lambda s, p: (0, s)),
                pl.BlockSpec((depth, tile), lambda s, p: (0, jnp.minimum(s, half - 1))),
                pl.BlockSpec((depth, tile), lambda s, p: (0, jnp.maximum(s - half, 0))),
            ],
            out_specs=whole((1024, 128)),
            scratch_shapes=[pltpu.VMEM((256, depth), BF16), pltpu.VMEM((256, 512), F32)],
        ),
        out_shape=jax.ShapeDtypeStruct((1024, 128), BF16),
        compiler_params=pltpu.CompilerParams(
            dimension_semantics=("arbitrary",), vmem_limit_bytes=40 * 2**20
        ),
        cost_estimate=pl.CostEstimate(
            flops=2 * 256 * 2 * rows * (depth + 512),
            bytes_accessed=4 * depth * rows + 2 * 256 * depth,
            transcendentals=depth,
        ),
        name="project",
    )(place, *blocks, energy, weight, own, other)


def finish_kernel(parts, out):
    total = jnp.sum(parts[...].astype(F32).reshape(128, 8, 128), axis=0)
    out[...] = jnp.concatenate([total[:, :64], total[:, 64:]], axis=0).T


def finish(parts):
    return pl.pallas_call(
        finish_kernel,
        out_shape=jax.ShapeDtypeStruct((64, 16), F32),
        compiler_params=pltpu.CompilerParams(vmem_limit_bytes=16 * 2**20),
        name="finish",
    )(parts)


def gather_trial(trial):
    xh, z = lax.axis_index("xh"), lax.axis_index("z")
    partner = shift(trial, "xh", 1)
    found = {(0, 0): trial, (1, 0): partner}
    for hop in range(1, 5):
        for k in range(2):
            if hop < 4 or k == 0:
                found[k, hop] = shift(found[k, hop - 1], "z", 1)
            if hop < 4 or k == 1:
                found[k, -hop] = shift(found[k, 1 - hop], "z", -1)
    places = [((xh + k) % 2) * 8 + (z - hop + 8) % 8 for k, hop in found]
    return jnp.stack(places).astype(jnp.int32), list(found.values())


def shards(rates, trial, test, col_energy, row_energy):
    own = rates.T
    other = shift(own, "core", 1)

    mine = (test.T.astype(F32) * jnp.exp(0.5 * row_energy)[None, :]).astype(BF16)
    pair = jnp.concatenate([mine, shift(mine, "core", 1)], axis=1)
    beside = shift(pair, "xl", 1)
    first = lax.axis_index("xl") == 0
    both = jnp.stack([jnp.where(first, pair, beside), jnp.where(first, beside, pair)])
    weight = lax.all_gather(both, "y", axis=1).reshape(512, -1)

    place, blocks = gather_trial(trial.T)
    parts = project(place, blocks, col_energy[None, :], weight, own, other)
    parts = lax.all_to_all(parts.reshape(128, 8, 128), PEERS, 0, 0)
    return finish(parts.reshape(1024, 128))


def solution(mesh):
    split = Mesh(mesh.devices.reshape(tuple(SIZES.values())), tuple(SIZES))
    placed = (P(ROW, COL), P(COL, ROW), P(ROW, COL), P(COL), P(ROW))
    return jax.shard_map(
        shards, mesh=split, in_specs=placed, out_specs=P(COL, ROW), check_vma=False
    )
```

```python
import jax
import jax.numpy as jnp
from jax import lax
from jax.experimental import pallas as pl
from jax.experimental.pallas import tpu as pltpu
from jax.sharding import Mesh
from jax.sharding import PartitionSpec as P

SIZES = {"xh": 2, "z": 8, "core": 2, "xl": 2, "y": 4}
ROW, COL = ("xh", "z", "core"), ("xl", "y")
PEERS = ("xh", "z", "xl", "y")
F32, BF16 = jnp.float32, jnp.bfloat16
NT = (((1,), (1,)), ((), ()))
MIB = 2**20


def shift(value, axis, by):
    n = SIZES[axis]
    return lax.ppermute(value, axis, [(i, (i + by) % n) for i in range(n)])


def rows_kernel(place, energy, *refs):
    pieces, rates, out, weight = refs[:4], *refs[4:]

    @pl.when(pl.program_id(0) == 0)
    def _():
        scale = jnp.exp(0.5 * energy[...])
        for n, piece in enumerate(pieces):
            for k in range(2):
                rows = pl.ds(pl.multiple_of(place[2 * n + k] * 64, 64), 64)
                block = piece[64 * k : 64 * k + 64, :].astype(F32) * scale
                weight[rows, :] = block.astype(BF16)

    product = lax.dot_general(rates[...], weight[...], NT, preferred_element_type=F32)
    out[...] = product.astype(BF16)


def sum_rows(place, energy, pieces, rates):
    depth, rows = rates.shape
    tile = 688
    whole = lambda shape: pl.BlockSpec(shape, lambda s, p: (0, 0))
    return pl.pallas_call(
        rows_kernel,
        grid_spec=pltpu.PrefetchScalarGridSpec(
            num_scalar_prefetch=1,
            grid=(pl.cdiv(depth, tile),),
            in_specs=[whole((1, rows))]
            + [whole((128, rows))] * 4
            + [pl.BlockSpec((tile, rows), lambda s, p: (s, 0))],
            out_specs=pl.BlockSpec((tile, 512), lambda s, p: (s, 0)),
            scratch_shapes=[pltpu.VMEM((512, rows), BF16)],
        ),
        out_shape=jax.ShapeDtypeStruct((depth, 512), BF16),
        compiler_params=pltpu.CompilerParams(
            dimension_semantics=("arbitrary",), vmem_limit_bytes=56 * MIB
        ),
        cost_estimate=pl.CostEstimate(
            flops=2 * rows * depth * 512,
            bytes_accessed=2 * depth * (rows + 512),
            transcendentals=rows,
        ),
        name="sum_rows",
    )(place, energy, *pieces, rates)


def columns_kernel(place, *refs):
    blocks, energy, own, other, own_tail, other_tail, out, total = refs[:16], *refs[16:]
    step, steps = pl.program_id(0), pl.num_programs(0)
    depth, tile = energy.shape[1], own.shape[0]

    def add(columns, left, right):
        scale = jnp.exp(-0.5 * energy[:, columns])
        basis = jnp.concatenate(
            [(block[:, columns].astype(F32) * scale).astype(BF16) for block in blocks], axis=0
        )
        both = (left[...].astype(F32) + right[...].astype(F32)).astype(BF16)
        total[...] += jnp.dot(basis, both, preferred_element_type=F32)

    @pl.when(step == 0)
    def _():
        total[...] = jnp.zeros_like(total)
        add(pl.ds(depth - own_tail.shape[0], own_tail.shape[0]), own_tail, other_tail)

    add(pl.ds(pl.multiple_of(step * tile, tile), tile), own, other)

    @pl.when(step == steps - 1)
    def _():
        left = lax.broadcasted_iota(jnp.int32, (8, 128), 1) < 64
        for n in range(16):
            for i in range(4):
                low = total[16 * n : 16 * n + 8, 128 * i : 128 * i + 128]
                high = total[16 * n + 8 : 16 * n + 16, 128 * i : 128 * i + 128]
                first = jnp.where(left, low, pltpu.roll(high, 64, 1))
                second = jnp.where(left, pltpu.roll(low, 64, 1), high)
                pair = jnp.concatenate([first, second], axis=0)
                rows = pl.ds(pl.multiple_of(place[n] * 64 + 16 * i, 16), 16)
                out[rows, :] = pair.astype(BF16)


def sum_columns(place, blocks, energy, own, other):
    depth = own.shape[0]
    tile, tail = 1024, depth % 1024
    whole = lambda shape: pl.BlockSpec(shape, lambda s, p: (0, 0))
    part = pl.BlockSpec((tile, 512), lambda s, p: (s, 0))
    last = pl.BlockSpec((tail, 512), lambda s, p: (depth // tail - 1, 0))
    return pl.pallas_call(
        columns_kernel,
        grid_spec=pltpu.PrefetchScalarGridSpec(
            num_scalar_prefetch=1,
            grid=(depth // tile,),
            in_specs=[whole((16, depth))] * 16 + [whole((1, depth)), part, part, last, last],
            out_specs=whole((1024, 128)),
            scratch_shapes=[pltpu.VMEM((256, 512), F32)],
        ),
        out_shape=jax.ShapeDtypeStruct((1024, 128), BF16),
        compiler_params=pltpu.CompilerParams(
            dimension_semantics=("arbitrary",), vmem_limit_bytes=24 * MIB
        ),
        cost_estimate=pl.CostEstimate(
            flops=2 * 256 * 512 * depth,
            bytes_accessed=4 * depth * 512 + 2 * 256 * depth,
            transcendentals=depth,
        ),
        name="sum_columns",
    )(place, *blocks, energy, own, other, own, other)


def finish_kernel(parts, out):
    total = jnp.sum(parts[...].astype(F32).reshape(128, 8, 128), axis=0)
    out[...] = jnp.concatenate([total[:, :64], total[:, 64:]], axis=0)


def finish(parts):
    return pl.pallas_call(
        finish_kernel,
        out_shape=jax.ShapeDtypeStruct((16, 64), F32),
        compiler_params=pltpu.CompilerParams(vmem_limit_bytes=8 * MIB),
        name="finish",
    )(parts).T


def after(value, *others):
    return lax.optimization_barrier((value, *others))[0]


def shards(rates, trial, test, col_energy, row_energy):
    trial, test = trial.T, test.T
    xh, z, xl, y = (lax.axis_index(axis) for axis in PEERS)

    found = {(0, 0): trial, (1, 0): shift(trial, "xh", 1)}
    found |= {(0, hop): shift(trial, "z", hop) for hop in (1, -1)}
    beside = shift(test, "xl", 1)

    pair = jnp.concatenate([test, beside], axis=0)
    pair = after(pair, found[0, 1], found[0, -1], found[1, 0])
    tests = {0: pair} | {hop: shift(pair, "y", hop) for hop in (1, -1, 2)}
    for hop in (1, 2, 3):
        for k in range(2):
            if (k, hop) not in found:
                found[k, hop] = shift(found[k, hop - 1], "z", 1)
                found[k, -hop] = shift(found[k, 1 - hop], "z", -1)
        if hop == 2:
            place = [((xl + k) % 2) * 4 + (y - n + 4) % 4 for n in tests for k in range(2)]
            place = jnp.stack(place).astype(jnp.int32)
            ready = [found[k, n] for k, n in ((0, 2), (0, -2), (1, 1), (1, -1))]
            place = after(place, *ready)
            own = sum_rows(place, row_energy[None, :], list(tests.values()), rates.T)
            other = shift(own, "core", 1)
    found[0, 4] = shift(found[0, 3], "z", 1)
    found[1, -4] = shift(found[1, -3], "z", -1)

    place = [((xh + k) % 2) * 8 + (z - hop + 8) % 8 for k, hop in found]
    place = jnp.stack(place).astype(jnp.int32)
    parts = sum_columns(place, list(found.values()), col_energy[None, :], own, other)
    parts = lax.all_to_all(parts.reshape(128, 8, 128), PEERS, 0, 0)
    return finish(parts.reshape(1024, 128))


def solution(mesh):
    split = Mesh(mesh.devices.reshape(tuple(SIZES.values())), tuple(SIZES))
    placed = (P(ROW, COL), P(COL, ROW), P(ROW, COL), P(COL), P(ROW))
    return jax.shard_map(
        shards, mesh=split, in_specs=placed, out_specs=P(COL, ROW), check_vma=False
    )
```

```python
import jax
import jax.numpy as jnp
from jax import lax
from jax.experimental import pallas as pl
from jax.experimental.pallas import tpu as pltpu
from jax.sharding import Mesh
from jax.sharding import PartitionSpec as P

SIZES = {"xh": 2, "z": 8, "core": 2, "xl": 2, "y": 4}
ROW, COL = ("xh", "z", "core"), ("xl", "y")
PEERS = ("xh", "z", "xl", "y")
F32, BF16 = jnp.float32, jnp.bfloat16
NT = (((1,), (1,)), ((), ()))
MIB = 2**20


def shift(value, axis, by):
    n = SIZES[axis]
    return lax.ppermute(value, axis, [(i, (i + by) % n) for i in range(n)])


def rows_kernel(place, energy, *refs):
    pieces, rates, out, weight = refs[:4], *refs[4:]

    @pl.when(pl.program_id(0) == 0)
    def _():
        scale = jnp.exp(0.5 * energy[...])
        for n, piece in enumerate(pieces):
            for k in range(2):
                rows = pl.ds(pl.multiple_of(place[2 * n + k] * 64, 64), 64)
                block = piece[64 * k : 64 * k + 64, :].astype(F32) * scale
                weight[rows, :] = block.astype(BF16)

    product = lax.dot_general(rates[...], weight[...], NT, preferred_element_type=F32)
    out[...] = product.astype(BF16)


def sum_rows(place, energy, pieces, rates):
    depth, rows = rates.shape
    tile = 1376
    whole = lambda shape: pl.BlockSpec(shape, lambda s, p: (0, 0))
    return pl.pallas_call(
        rows_kernel,
        grid_spec=pltpu.PrefetchScalarGridSpec(
            num_scalar_prefetch=1,
            grid=(pl.cdiv(depth, tile),),
            in_specs=[whole((1, rows))]
            + [whole((128, rows))] * 4
            + [pl.BlockSpec((tile, rows), lambda s, p: (s, 0))],
            out_specs=pl.BlockSpec((tile, 512), lambda s, p: (s, 0)),
            scratch_shapes=[pltpu.VMEM((512, rows), BF16)],
        ),
        out_shape=jax.ShapeDtypeStruct((depth, 512), BF16),
        compiler_params=pltpu.CompilerParams(
            dimension_semantics=("arbitrary",), vmem_limit_bytes=56 * MIB
        ),
        cost_estimate=pl.CostEstimate(
            flops=2 * rows * depth * 512,
            bytes_accessed=2 * depth * (rows + 512),
            transcendentals=rows,
        ),
        name="sum_rows",
    )(place, energy, *pieces, rates)


def columns_kernel(place, *refs):
    blocks, energy, own, other, own_tail, other_tail, out, total = refs[:9], *refs[9:]
    step, steps = pl.program_id(0), pl.num_programs(0)
    depth, tile = energy.shape[1], own.shape[0]

    def add(columns, left, right):
        scale = jnp.exp(-0.5 * energy[:, columns])
        basis = jnp.concatenate(
            [(block[:, columns].astype(F32) * scale).astype(BF16) for block in blocks], axis=0
        )
        both = (left[...].astype(F32) + right[...].astype(F32)).astype(BF16)
        total[...] += jnp.dot(basis, both, preferred_element_type=F32)

    @pl.when(step == 0)
    def _():
        total[...] = jnp.zeros_like(total)
        add(pl.ds(depth - own_tail.shape[0], own_tail.shape[0]), own_tail, other_tail)

    add(pl.ds(pl.multiple_of(step * tile, tile), tile), own, other)

    @pl.when(step == steps - 1)
    def _():
        left = lax.broadcasted_iota(jnp.int32, (8, 128), 1) < 64
        for n in range(16):
            for i in range(4):
                low = total[16 * n : 16 * n + 8, 128 * i : 128 * i + 128]
                high = total[16 * n + 8 : 16 * n + 16, 128 * i : 128 * i + 128]
                first = jnp.where(left, low, pltpu.roll(high, 64, 1))
                second = jnp.where(left, pltpu.roll(low, 64, 1), high)
                pair = jnp.concatenate([first, second], axis=0)
                rows = pl.ds(pl.multiple_of(place[n] * 64 + 16 * i, 16), 16)
                out[rows, :] = pair.astype(BF16)


def sum_columns(place, blocks, energy, own, other):
    depth = own.shape[0]
    tile, tail = 1024, depth % 1024
    whole = lambda shape: pl.BlockSpec(shape, lambda s, p: (0, 0))
    part = pl.BlockSpec((tile, 512), lambda s, p: (s, 0))
    last = pl.BlockSpec((tail, 512), lambda s, p: (depth // tail - 1, 0))
    return pl.pallas_call(
        columns_kernel,
        grid_spec=pltpu.PrefetchScalarGridSpec(
            num_scalar_prefetch=1,
            grid=(depth // tile,),
            in_specs=[whole(block.shape) for block in blocks]
            + [whole((1, depth)), part, part, last, last],
            out_specs=whole((1024, 128)),
            scratch_shapes=[pltpu.VMEM((256, 512), F32)],
        ),
        out_shape=jax.ShapeDtypeStruct((1024, 128), BF16),
        compiler_params=pltpu.CompilerParams(
            dimension_semantics=("arbitrary",), vmem_limit_bytes=60 * MIB
        ),
        cost_estimate=pl.CostEstimate(
            flops=2 * 256 * 512 * depth,
            bytes_accessed=4 * depth * 512 + 2 * 256 * depth,
            transcendentals=depth,
        ),
        name="sum_columns",
    )(place, *blocks, energy, own, other, own, other)


def finish_kernel(parts, out):
    total = jnp.sum(parts[...].astype(F32).reshape(128, 8, 128), axis=0)
    out[...] = jnp.concatenate([total[:, :64], total[:, 64:]], axis=0)


def finish(parts):
    return pl.pallas_call(
        finish_kernel,
        out_shape=jax.ShapeDtypeStruct((16, 64), F32),
        compiler_params=pltpu.CompilerParams(vmem_limit_bytes=8 * MIB),
        name="finish",
    )(parts).T


def after(value, *others):
    return lax.optimization_barrier((value, *others))[0]


def shards(rates, trial, test, col_energy, row_energy):
    trial, test = trial.T, test.T
    xh, z, xl, y = (lax.axis_index(axis) for axis in PEERS)

    held = {0: jnp.concatenate([trial, shift(trial, "xh", 1)], axis=0)}
    pair = jnp.concatenate([test, shift(test, "xl", 1)], axis=0)
    tests = {0: pair} | {hop: shift(pair, "y", hop) for hop in (1, -1, 2)}
    for hop in (1, 2, 3):
        held[hop] = shift(held[hop - 1], "z", 1)
        held[-hop] = shift(held[1 - hop], "z", -1)
        if hop == 1:
            place = [((xl + k) % 2) * 4 + (y - n + 4) % 4 for n in tests for k in range(2)]
            place = after(jnp.stack(place).astype(jnp.int32), held[1], held[-1])
            own = sum_rows(place, row_energy[None, :], list(tests.values()), rates.T)
        if hop == 2:
            other = shift(after(own, held[2], held[-2]), "core", 1)
    held[4] = shift(held[3][:16], "z", 1)
    held[-4] = shift(held[-3][16:], "z", -1)

    place = [((xh + k) % 2) * 8 + (z - hop + 8) % 8 for hop in held for k in range(2)]
    place = jnp.stack(place[:15] + place[17:]).astype(jnp.int32)
    parts = sum_columns(place, list(held.values()), col_energy[None, :], own, other)
    parts = lax.all_to_all(parts.reshape(128, 8, 128), PEERS, 0, 0)
    return finish(parts.reshape(1024, 128))


def solution(mesh):
    split = Mesh(mesh.devices.reshape(tuple(SIZES.values())), tuple(SIZES))
    placed = (P(ROW, COL), P(COL, ROW), P(ROW, COL), P(COL), P(ROW))
    return jax.shard_map(
        shards, mesh=split, in_specs=placed, out_specs=P(COL, ROW), check_vma=False
    )
```

```python
import jax
import jax.numpy as jnp
from jax import lax
from jax.experimental import pallas as pl
from jax.experimental.pallas import tpu as pltpu
from jax.sharding import Mesh
from jax.sharding import PartitionSpec as P

SIZES = {"xh": 2, "z": 8, "core": 2, "xl": 2, "y": 4}
ROW, COL = ("xh", "z", "core"), ("xl", "y")
PEERS = ("xh", "z", "xl", "y")
F32, BF16 = jnp.float32, jnp.bfloat16
NT = (((1,), (1,)), ((), ()))
MIB = 2**20


def shift(value, axis, by):
    n = SIZES[axis]
    return lax.ppermute(value, axis, [(i, (i + by) % n) for i in range(n)])


def join_kernel(first, second, out):
    out[...] = jnp.concatenate([first[...], second[...]], axis=0)


def join(first, second):
    rows, columns = first.shape
    return pl.pallas_call(
        join_kernel,
        out_shape=jax.ShapeDtypeStruct((2 * rows, columns), first.dtype),
        compiler_params=pltpu.CompilerParams(vmem_limit_bytes=8 * MIB),
        name="join",
    )(first, second)


def pack_kernel(place, energy, *refs):
    pieces, out = refs[:-1], refs[-1]
    scale = jnp.exp(0.5 * energy[...])
    for n, piece in enumerate(pieces):
        for k in range(2):
            rows = pl.ds(pl.multiple_of(place[2 * n + k] * 64, 64), 64)
            out[rows, :] = (piece[64 * k : 64 * k + 64, :].astype(F32) * scale).astype(BF16)


def pack(place, energy, pieces):
    whole = pl.BlockSpec(memory_space=pltpu.VMEM)
    return pl.pallas_call(
        pack_kernel,
        in_specs=[pl.BlockSpec(memory_space=pltpu.SMEM)] + [whole] * (1 + len(pieces)),
        out_specs=whole,
        out_shape=jax.ShapeDtypeStruct((512, energy.shape[1]), BF16),
        compiler_params=pltpu.CompilerParams(vmem_limit_bytes=8 * MIB),
        name="pack",
    )(place, energy, *pieces)


def rows_kernel(weight, rates, *refs):
    def product(block):
        total = lax.dot_general(block[...], weight[...], NT, preferred_element_type=F32)
        return total.astype(BF16)

    if len(refs) == 1:
        refs[0][...] = product(rates)
        return
    tail, out = refs
    step, steps, tile = pl.program_id(0), pl.num_programs(0), rates.shape[0]
    out[pl.ds(pl.multiple_of(step * tile, tile), tile), :] = product(rates)

    @pl.when(step == steps - 1)
    def _():
        out[out.shape[0] - tail.shape[0] :, :] = product(tail)


def sum_rows(weight, rates, start, stop):
    rows, tile = rates.shape[1], 1024
    size, tail = stop - start, (stop - start) % tile
    in_specs = [
        pl.BlockSpec((512, rows), lambda s: (0, 0)),
        pl.BlockSpec((tile, rows), lambda s: (s + start // tile, 0)),
    ]
    out_specs = pl.BlockSpec((tile, 512), lambda s: (s, 0))
    if tail:
        in_specs += [pl.BlockSpec((tail, rows), lambda s: (stop // tail - 1, 0))]
        out_specs = pl.BlockSpec((size, 512), lambda s: (0, 0))
    return pl.pallas_call(
        rows_kernel,
        grid=(size // tile,),
        in_specs=in_specs,
        out_specs=out_specs,
        out_shape=jax.ShapeDtypeStruct((size, 512), BF16),
        compiler_params=pltpu.CompilerParams(
            dimension_semantics=("arbitrary",), vmem_limit_bytes=48 * MIB
        ),
        cost_estimate=pl.CostEstimate(
            flops=2 * rows * size * 512,
            bytes_accessed=2 * size * (rows + 512),
            transcendentals=0,
        ),
        name="sum_rows",
    )(weight, *[rates] * (len(in_specs) - 1))


def columns_kernel(place, *refs):
    blocks, energy, first, second, tail = refs[:9], refs[9], refs[10:12], refs[12:14], refs[14:16]
    out, total = refs[16:]
    step, steps = pl.program_id(0), pl.num_programs(0)
    depth, tile = energy.shape[1], first[0].shape[0]

    def add(columns, left, right):
        scale = jnp.exp(-0.5 * energy[:, columns])
        basis = jnp.concatenate(
            [(block[:, columns].astype(F32) * scale).astype(BF16) for block in blocks], axis=0
        )
        both = (left[...].astype(F32) + right[...].astype(F32)).astype(BF16)
        total[...] += jnp.dot(basis, both, preferred_element_type=F32)

    columns = pl.ds(pl.multiple_of(step * tile, tile), tile)

    @pl.when(step == 0)
    def _():
        total[...] = jnp.zeros_like(total)
        size = tail[0].shape[0]
        add(pl.ds(depth - size, size), *tail)

    @pl.when(step < steps // 2)
    def _():
        add(columns, *first)

    @pl.when(step >= steps // 2)
    def _():
        add(columns, *second)

    @pl.when(step == steps - 1)
    def _():
        left = lax.broadcasted_iota(jnp.int32, (8, 128), 1) < 64
        for n in range(16):
            for i in range(4):
                low = total[16 * n : 16 * n + 8, 128 * i : 128 * i + 128]
                high = total[16 * n + 8 : 16 * n + 16, 128 * i : 128 * i + 128]
                first = jnp.where(left, low, pltpu.roll(high, 64, 1))
                second = jnp.where(left, pltpu.roll(low, 64, 1), high)
                pair = jnp.concatenate([first, second], axis=0)
                rows = pl.ds(pl.multiple_of(place[n] * 64 + 16 * i, 16), 16)
                out[rows, :] = pair.astype(BF16)


def sum_columns(place, blocks, energy, first, second):
    depth, tile = energy.shape[1], 1024
    tail, half = depth % tile, depth // tile // 2
    whole = lambda shape: pl.BlockSpec(shape, lambda s, p: (0, 0))
    early = pl.BlockSpec((tile, 512), lambda s, p: (jnp.minimum(s, half - 1), 0))
    late = pl.BlockSpec((tile, 512), lambda s, p: (jnp.maximum(s - half, 0), 0))
    last = pl.BlockSpec((tail, 512), lambda s, p: (half * tile // tail, 0))
    return pl.pallas_call(
        columns_kernel,
        grid_spec=pltpu.PrefetchScalarGridSpec(
            num_scalar_prefetch=1,
            grid=(2 * half,),
            in_specs=[whole(block.shape) for block in blocks]
            + [whole((1, depth)), early, early, late, late, last, last],
            out_specs=whole((1024, 128)),
            scratch_shapes=[pltpu.VMEM((256, 512), F32)],
        ),
        out_shape=jax.ShapeDtypeStruct((1024, 128), BF16),
        compiler_params=pltpu.CompilerParams(
            dimension_semantics=("arbitrary",), vmem_limit_bytes=24 * MIB
        ),
        cost_estimate=pl.CostEstimate(
            flops=2 * 256 * 512 * depth,
            bytes_accessed=4 * depth * 512 + 2 * 256 * depth,
            transcendentals=depth,
        ),
        name="sum_columns",
    )(place, *blocks, energy, *first, *second, *second)


def finish_kernel(parts, out):
    total = jnp.sum(parts[...].astype(F32).reshape(128, 8, 128), axis=0)
    out[...] = jnp.concatenate([total[:, :64], total[:, 64:]], axis=0)


def finish(parts):
    return pl.pallas_call(
        finish_kernel,
        out_shape=jax.ShapeDtypeStruct((16, 64), F32),
        compiler_params=pltpu.CompilerParams(vmem_limit_bytes=8 * MIB),
        name="finish",
    )(parts).T


def together(*values):
    return lax.optimization_barrier(values)


def after(value, *others):
    return lax.optimization_barrier((value, *others))[0]


def shards(rates, trial, test, col_energy, row_energy):
    trial, test = trial.T, test.T
    xh, z, xl, y = (lax.axis_index(axis) for axis in PEERS)

    def hops(n):
        return shift(held[n - 1], "z", 1), shift(held[1 - n], "z", -1)

    partner, beside = together(shift(trial, "xh", 1), shift(test, "xl", 1))
    held, tests = {0: join(trial, partner)}, {0: join(test, beside)}

    sent = hops(1) + tuple(shift(tests[0], "y", hop) for hop in (1, -1))
    held[1], held[-1], tests[1], tests[-1] = together(*sent)

    held[2], held[-2], tests[2] = together(*hops(2), shift(after(tests[0], held[1]), "y", 2))

    place = [((xl + k) % 2) * 4 + (y - n + 4) % 4 for n in tests for k in range(2)]
    place = after(jnp.stack(place).astype(jnp.int32), held[2], held[-2])
    weight = pack(place, row_energy[None, :], list(tests.values()))
    depth = rates.shape[1]
    cut = depth // 2048 // 2 * 2048
    first = sum_rows(weight, rates.T, 0, cut)
    second = sum_rows(after(weight, first), rates.T, cut, depth)
    held[3], held[-3], second = together(*hops(3), second)

    first, second = ((part, shift(part, "core", 1)) for part in (first, second))
    held[4] = shift(held[3][:16], "z", 1)
    held[-4] = shift(held[-3][16:], "z", -1)

    place = [((xh + k) % 2) * 8 + (z - hop + 8) % 8 for hop in held for k in range(2)]
    place = jnp.stack(place[:15] + place[17:]).astype(jnp.int32)
    parts = sum_columns(place, list(held.values()), col_energy[None, :], first, second)
    parts = lax.all_to_all(parts.reshape(128, 8, 128), PEERS, 0, 0)
    return finish(parts.reshape(1024, 128))


def solution(mesh):
    split = Mesh(mesh.devices.reshape(tuple(SIZES.values())), tuple(SIZES))
    placed = (P(ROW, COL), P(COL, ROW), P(ROW, COL), P(COL), P(ROW))
    return jax.shard_map(
        shards, mesh=split, in_specs=placed, out_specs=P(COL, ROW), check_vma=False
    )
```

```python
import jax
import jax.numpy as jnp
from jax import lax
from jax.experimental import pallas as pl
from jax.experimental.pallas import tpu as pltpu
from jax.sharding import Mesh
from jax.sharding import PartitionSpec as P

SIZES = {"xh": 2, "z": 8, "core": 2, "xl": 2, "y": 4}
ROW, COL = ("xh", "z", "core"), ("xl", "y")
PEERS = ("xh", "z", "xl", "y")
F32, BF16 = jnp.float32, jnp.bfloat16
NT = (((1,), (1,)), ((), ()))
MIB = 2**20


def swap(value, axis, side=0):
    n = SIZES[axis]
    pairs = [((i + side) % n, (i + 1 + side) % n) for i in range(0, n, 2)]
    return lax.ppermute(value, axis, pairs + [(b, a) for a, b in pairs])


def cross(value, axis):
    n = SIZES[axis]
    return lax.ppermute(value, axis, [(i, (i + n // 2) % n) for i in range(n)])


def join_kernel(first, second, out):
    out[...] = jnp.concatenate([first[...], second[...]], axis=0)


def join(first, second):
    rows, columns = first.shape
    return pl.pallas_call(
        join_kernel,
        out_shape=jax.ShapeDtypeStruct((2 * rows, columns), first.dtype),
        compiler_params=pltpu.CompilerParams(vmem_limit_bytes=8 * MIB),
        name="join",
    )(first, second)


def pack_kernel(place, energy, *refs):
    pieces, out = refs[:-1], refs[-1]
    scale = jnp.exp(0.5 * energy[...])
    for n, piece in enumerate(pieces):
        for k in range(2):
            rows = pl.ds(pl.multiple_of(place[2 * n + k] * 64, 64), 64)
            out[rows, :] = (piece[64 * k : 64 * k + 64, :].astype(F32) * scale).astype(BF16)


def pack(place, energy, pieces):
    whole = pl.BlockSpec(memory_space=pltpu.VMEM)
    return pl.pallas_call(
        pack_kernel,
        in_specs=[pl.BlockSpec(memory_space=pltpu.SMEM)] + [whole] * (1 + len(pieces)),
        out_specs=whole,
        out_shape=jax.ShapeDtypeStruct((512, energy.shape[1]), BF16),
        compiler_params=pltpu.CompilerParams(vmem_limit_bytes=8 * MIB),
        name="pack",
    )(place, energy, *pieces)


def rows_kernel(weight, rates, *refs):
    def product(block):
        total = lax.dot_general(block[...], weight[...], NT, preferred_element_type=F32)
        return total.astype(BF16)

    if len(refs) == 1:
        refs[0][...] = product(rates)
        return
    tail, out = refs
    step, steps, tile = pl.program_id(0), pl.num_programs(0), rates.shape[0]
    out[pl.ds(pl.multiple_of(step * tile, tile), tile), :] = product(rates)

    @pl.when(step == steps - 1)
    def _():
        out[out.shape[0] - tail.shape[0] :, :] = product(tail)


def sum_rows(weight, rates, start, stop):
    rows, tile = rates.shape[1], 1024
    size, tail = stop - start, (stop - start) % tile
    in_specs = [
        pl.BlockSpec((512, rows), lambda s: (0, 0)),
        pl.BlockSpec((tile, rows), lambda s: (s + start // tile, 0)),
    ]
    out_specs = pl.BlockSpec((tile, 512), lambda s: (s, 0))
    if tail:
        in_specs += [pl.BlockSpec((tail, rows), lambda s: (stop // tail - 1, 0))]
        out_specs = pl.BlockSpec((size, 512), lambda s: (0, 0))
    return pl.pallas_call(
        rows_kernel,
        grid=(size // tile,),
        in_specs=in_specs,
        out_specs=out_specs,
        out_shape=jax.ShapeDtypeStruct((size, 512), BF16),
        compiler_params=pltpu.CompilerParams(
            dimension_semantics=("arbitrary",), vmem_limit_bytes=48 * MIB
        ),
        cost_estimate=pl.CostEstimate(
            flops=2 * rows * size * 512,
            bytes_accessed=2 * size * (rows + 512),
            transcendentals=0,
        ),
        name="sum_rows",
    )(weight, *[rates] * (len(in_specs) - 1))


def columns_kernel(place, *refs):
    blocks, energy, first, second, tail = refs[:8], refs[8], refs[9:11], refs[11:13], refs[13:15]
    out, total = refs[15:]
    step, steps = pl.program_id(0), pl.num_programs(0)
    depth, tile = energy.shape[1], first[0].shape[0]

    def add(columns, left, right):
        scale = jnp.exp(-0.5 * energy[:, columns])
        basis = jnp.concatenate(
            [(block[:, columns].astype(F32) * scale).astype(BF16) for block in blocks], axis=0
        )
        both = (left[...].astype(F32) + right[...].astype(F32)).astype(BF16)
        total[...] += jnp.dot(basis, both, preferred_element_type=F32)

    columns = pl.ds(pl.multiple_of(step * tile, tile), tile)

    @pl.when(step == 0)
    def _():
        total[...] = jnp.zeros_like(total)
        size = tail[0].shape[0]
        add(pl.ds(depth - size, size), *tail)

    @pl.when(step < steps // 2)
    def _():
        add(columns, *first)

    @pl.when(step >= steps // 2)
    def _():
        add(columns, *second)

    @pl.when(step == steps - 1)
    def _():
        left = lax.broadcasted_iota(jnp.int32, (8, 128), 1) < 64
        for n in range(16):
            for i in range(4):
                low = total[16 * n : 16 * n + 8, 128 * i : 128 * i + 128]
                high = total[16 * n + 8 : 16 * n + 16, 128 * i : 128 * i + 128]
                first = jnp.where(left, low, pltpu.roll(high, 64, 1))
                second = jnp.where(left, pltpu.roll(low, 64, 1), high)
                pair = jnp.concatenate([first, second], axis=0)
                rows = pl.ds(pl.multiple_of(place[n] * 64 + 16 * i, 16), 16)
                out[rows, :] = pair.astype(BF16)


def sum_columns(place, blocks, energy, first, second):
    depth, tile = energy.shape[1], 1024
    tail, half = depth % tile, depth // tile // 2
    whole = lambda shape: pl.BlockSpec(shape, lambda s, p: (0, 0))
    early = pl.BlockSpec((tile, 512), lambda s, p: (jnp.minimum(s, half - 1), 0))
    late = pl.BlockSpec((tile, 512), lambda s, p: (jnp.maximum(s - half, 0), 0))
    last = pl.BlockSpec((tail, 512), lambda s, p: (half * tile // tail, 0))
    return pl.pallas_call(
        columns_kernel,
        grid_spec=pltpu.PrefetchScalarGridSpec(
            num_scalar_prefetch=1,
            grid=(2 * half,),
            in_specs=[whole(block.shape) for block in blocks]
            + [whole((1, depth)), early, early, late, late, last, last],
            out_specs=whole((1024, 128)),
            scratch_shapes=[pltpu.VMEM((256, 512), F32)],
        ),
        out_shape=jax.ShapeDtypeStruct((1024, 128), BF16),
        compiler_params=pltpu.CompilerParams(
            dimension_semantics=("arbitrary",), vmem_limit_bytes=24 * MIB
        ),
        cost_estimate=pl.CostEstimate(
            flops=2 * 256 * 512 * depth,
            bytes_accessed=4 * depth * 512 + 2 * 256 * depth,
            transcendentals=depth,
        ),
        name="sum_columns",
    )(place, *blocks, energy, *first, *second, *second)


def finish_kernel(parts, out):
    total = jnp.sum(parts[...].astype(F32).reshape(128, 8, 128), axis=0)
    out[...] = jnp.concatenate([total[:, :64], total[:, 64:]], axis=0)


def finish(parts):
    return pl.pallas_call(
        finish_kernel,
        out_shape=jax.ShapeDtypeStruct((16, 64), F32),
        compiler_params=pltpu.CompilerParams(vmem_limit_bytes=8 * MIB),
        name="finish",
    )(parts).T


def together(*values):
    return lax.optimization_barrier(values)


def after(value, *others):
    return lax.optimization_barrier((value, *others))[0]


def shards(rates, trial, test, col_energy, row_energy):
    trial, test = trial.T, test.T
    xh, z, xl, y = (lax.axis_index(axis) for axis in PEERS)

    def hops(n):
        return swap(held[1 - n], "z"), swap(held[n - 1], "z", 1)

    partner, beside = together(swap(trial, "xh"), swap(test, "xl"))
    held, tests = {0: join(trial, partner)}, {0: join(test, beside)}

    sent = hops(1) + (swap(tests[0], "y"), swap(tests[0], "y", 1))
    held[1], held[-1], tests[1], tests[-1] = together(*sent)

    held[2], held[-2], tests[2] = together(*hops(2), cross(after(tests[0], held[1]), "y"))

    sign_y, sign_z = 1 - 2 * (y % 2), 1 - 2 * (z % 2)
    place = [((xl + k) % 2) * 4 + (y + n * sign_y + 4) % 4 for n in tests for k in range(2)]
    place = after(jnp.stack(place).astype(jnp.int32), held[2], held[-2])
    weight = pack(place, row_energy[None, :], list(tests.values()))
    depth = rates.shape[1]
    cut = depth // 2048 // 2 * 2048
    first = sum_rows(weight, rates.T, 0, cut)
    second = sum_rows(after(weight, first), rates.T, cut, depth)
    held[3], held[-3], second = together(*hops(3), second)

    first, second = ((part, swap(part, "core")) for part in (first, second))
    held[4] = swap(held[-3], "z")

    place = [((xh + k) % 2) * 8 + (z + n * sign_z + 8) % 8 for n in held for k in range(2)]
    place = jnp.stack(place).astype(jnp.int32)
    parts = sum_columns(place, list(held.values()), col_energy[None, :], first, second)
    parts = lax.all_to_all(parts.reshape(128, 8, 128), PEERS, 0, 0)
    return finish(parts.reshape(1024, 128))


def solution(mesh):
    split = Mesh(mesh.devices.reshape(tuple(SIZES.values())), tuple(SIZES))
    placed = (P(ROW, COL), P(COL, ROW), P(ROW, COL), P(COL), P(ROW))
    return jax.shard_map(
        shards, mesh=split, in_specs=placed, out_specs=P(COL, ROW), check_vma=False
    )
```

```python
import jax
import jax.numpy as jnp
from jax import lax
from jax.experimental import pallas as pl
from jax.experimental.pallas import tpu as pltpu
from jax.sharding import Mesh
from jax.sharding import PartitionSpec as P

SIZES = {"xh": 2, "z": 8, "core": 2, "xl": 2, "y": 4}
ROW, COL = ("xh", "z", "core"), ("xl", "y")
PEERS = ("xh", "z", "xl", "y")
F32, BF16 = jnp.float32, jnp.bfloat16
NT = (((1,), (1,)), ((), ()))
MIB = 2**20


def swap(value, axis, side=0):
    n = SIZES[axis]
    pairs = [((i + side) % n, (i + 1 + side) % n) for i in range(0, n, 2)]
    return lax.ppermute(value, axis, pairs + [(b, a) for a, b in pairs])


def cross(value, axis):
    n = SIZES[axis]
    return lax.ppermute(value, axis, [(i, (i + n // 2) % n) for i in range(n)])


def together(*values):
    return lax.optimization_barrier(values)


def join_kernel(first, second, out):
    out[...] = jnp.concatenate([first[...], second[...]], axis=0)


def join(first, second):
    rows, columns = first.shape
    return pl.pallas_call(
        join_kernel,
        out_shape=jax.ShapeDtypeStruct((2 * rows, columns), first.dtype),
        compiler_params=pltpu.CompilerParams(vmem_limit_bytes=8 * MIB),
        name="join",
    )(first, second)


def pack_kernel(place, energy, *refs):
    pieces, out = refs[:-1], refs[-1]
    scale = jnp.exp(0.5 * energy[...])
    for n, piece in enumerate(pieces):
        rows = pl.ds(pl.multiple_of(place[n] * 64, 64), 64)
        out[rows, :] = (piece[...].astype(F32) * scale).astype(BF16)


def pack(place, energy, pieces):
    whole = pl.BlockSpec(memory_space=pltpu.VMEM)
    return pl.pallas_call(
        pack_kernel,
        in_specs=[pl.BlockSpec(memory_space=pltpu.SMEM)] + [whole] * (1 + len(pieces)),
        out_specs=whole,
        out_shape=jax.ShapeDtypeStruct((256, energy.shape[1]), BF16),
        compiler_params=pltpu.CompilerParams(vmem_limit_bytes=8 * MIB),
        name="pack",
    )(place, energy, *pieces)


def rows_kernel(weight, rates, out):
    total = lax.dot_general(rates[...], weight[...], NT, preferred_element_type=F32)
    out[...] = total.astype(BF16)


def sum_rows(weight, rates):
    (depth, rows), columns = rates.shape, weight.shape[0]
    tile = 1376
    return pl.pallas_call(
        rows_kernel,
        grid=(pl.cdiv(depth, tile),),
        in_specs=[
            pl.BlockSpec((columns, rows), lambda s: (0, 0)),
            pl.BlockSpec((tile, rows), lambda s: (s, 0)),
        ],
        out_specs=pl.BlockSpec((tile, columns), lambda s: (s, 0)),
        out_shape=jax.ShapeDtypeStruct((depth, columns), BF16),
        compiler_params=pltpu.CompilerParams(
            dimension_semantics=("arbitrary",), vmem_limit_bytes=48 * MIB
        ),
        cost_estimate=pl.CostEstimate(
            flops=2 * rows * depth * columns,
            bytes_accessed=2 * depth * (rows + columns),
            transcendentals=0,
        ),
        name="sum_rows",
    )(weight, rates)


def columns_kernel(place, *refs):
    blocks, energy, pairs, out, total = refs[:8], refs[8], (refs[9:11], refs[11:13]), *refs[13:]
    depth, tile = energy.shape[1], 1024

    for start in range(0, depth, tile):
        part = slice(start, min(start + tile, depth))
        scale = jnp.exp(-0.5 * energy[:, part])
        basis = jnp.concatenate(
            [(block[:, part].astype(F32) * scale).astype(BF16) for block in blocks], axis=0
        )
        for k, (left, right) in enumerate(pairs):
            both = (left[part, :].astype(F32) + right[part, :].astype(F32)).astype(BF16)
            product = jnp.dot(basis, both, preferred_element_type=F32)
            half = slice(256 * k, 256 * k + 256)
            total[:, half] = product if start == 0 else total[:, half] + product

    left = lax.broadcasted_iota(jnp.int32, (8, 128), 1) < 64
    for n in range(16):
        for i in range(4):
            low = total[16 * n : 16 * n + 8, 128 * i : 128 * i + 128]
            high = total[16 * n + 8 : 16 * n + 16, 128 * i : 128 * i + 128]
            first = jnp.where(left, low, pltpu.roll(high, 64, 1))
            second = jnp.where(left, pltpu.roll(low, 64, 1), high)
            pair = jnp.concatenate([first, second], axis=0)
            to = place[n] * 64 + place[16 + i // 2] * 32 + 16 * (i % 2)
            out[pl.ds(pl.multiple_of(to, 16), 16), :] = pair.astype(BF16)


def sum_columns(place, blocks, energy, pairs):
    depth = energy.shape[1]
    whole = pl.BlockSpec(memory_space=pltpu.VMEM)
    return pl.pallas_call(
        columns_kernel,
        in_specs=[pl.BlockSpec(memory_space=pltpu.SMEM)] + [whole] * (len(blocks) + 5),
        out_specs=whole,
        out_shape=jax.ShapeDtypeStruct((1024, 128), BF16),
        scratch_shapes=[pltpu.VMEM((256, 512), F32)],
        compiler_params=pltpu.CompilerParams(vmem_limit_bytes=24 * MIB),
        cost_estimate=pl.CostEstimate(
            flops=2 * 256 * 512 * depth,
            bytes_accessed=4 * depth * 512 + 2 * 256 * depth,
            transcendentals=depth,
        ),
        name="sum_columns",
    )(place, *blocks, energy, *pairs[0], *pairs[1])


def finish_kernel(parts, out):
    total = jnp.sum(parts[...].astype(F32).reshape(128, 8, 128), axis=0)
    out[...] = jnp.concatenate([total[:, :64], total[:, 64:]], axis=0)


def finish(parts):
    return pl.pallas_call(
        finish_kernel,
        out_shape=jax.ShapeDtypeStruct((16, 64), F32),
        compiler_params=pltpu.CompilerParams(vmem_limit_bytes=8 * MIB),
        name="finish",
    )(parts).T


def shards(rates, trial, test, col_energy, row_energy):
    rates, trial, test = rates.T, trial.T, test.T
    xh, z, xl, y = (lax.axis_index(axis) for axis in PEERS)
    sign_y, sign_z = 1 - 2 * (y % 2), 1 - 2 * (z % 2)

    partner, *tests = together(
        swap(trial, "xh"), swap(test, "y"), swap(test, "y", 1), cross(test, "y")
    )
    place = jnp.stack([(y + h * sign_y + 4) % 4 for h in (0, 1, -1, 2)]).astype(jnp.int32)
    weight = pack(place, row_energy[None, :], [test, *tests])
    beside = swap(weight, "xl")
    near = sum_rows(weight, rates)

    held = {0: join(trial, partner)}

    def hops(n):
        return swap(held[1 - n], "z"), swap(held[n - 1], "z", 1)

    held[1], held[-1], near = together(*hops(1), near)
    far = sum_rows(together(beside, held[1])[0], rates)
    held[2], held[-2], far = together(*hops(2), far)
    near, far = ((part, swap(part, "core")) for part in (near, far))
    held[3], held[-3] = together(*hops(3))
    held[4] = swap(held[-3], "z")

    place = [((xh + k) % 2) * 8 + (z + h * sign_z + 8) % 8 for h in held for k in range(2)]
    place = jnp.stack([*place, xl, 1 - xl]).astype(jnp.int32)
    parts = sum_columns(place, list(held.values()), col_energy[None, :], (near, far))
    parts = lax.all_to_all(parts.reshape(128, 8, 128), PEERS, 0, 0)
    return finish(parts.reshape(1024, 128))


def solution(mesh):
    split = Mesh(mesh.devices.reshape(tuple(SIZES.values())), tuple(SIZES))
    placed = (P(ROW, COL), P(COL, ROW), P(ROW, COL), P(COL), P(ROW))
    return jax.shard_map(
        shards, mesh=split, in_specs=placed, out_specs=P(COL, ROW), check_vma=False
    )
```

```python
import jax
import jax.numpy as jnp
from jax import lax
from jax.experimental import pallas as pl
from jax.experimental.pallas import tpu as pltpu
from jax.sharding import Mesh
from jax.sharding import PartitionSpec as P

SIZES = {"xh": 2, "z": 8, "core": 2, "xl": 2, "y": 4}
ROW, COL = ("xh", "z", "core"), ("xl", "y")
PEERS = ("xh", "z", "xl", "y")
F32, BF16 = jnp.float32, jnp.bfloat16
NT = (((1,), (1,)), ((), ()))
MIB = 2**20


def swap(value, axis, side=0):
    n = SIZES[axis]
    pairs = [((i + side) % n, (i + 1 + side) % n) for i in range(0, n, 2)]
    return lax.ppermute(value, axis, pairs + [(b, a) for a, b in pairs])


def cross(value, axis):
    n = SIZES[axis]
    return lax.ppermute(value, axis, [(i, (i + n // 2) % n) for i in range(n)])


def together(*values):
    return lax.optimization_barrier(values)


def after(value, *others):
    return together(value, *others)[0]


def join_kernel(first, second, out):
    out[...] = jnp.concatenate([first[...], second[...]], axis=0)


def join(first, second):
    rows, columns = first.shape
    return pl.pallas_call(
        join_kernel,
        out_shape=jax.ShapeDtypeStruct((2 * rows, columns), first.dtype),
        compiler_params=pltpu.CompilerParams(vmem_limit_bytes=8 * MIB),
        name="join",
    )(first, second)


def hold_kernel(value, out):
    out[...] = value[...]


def hold(value):
    return pl.pallas_call(
        hold_kernel,
        out_shape=jax.ShapeDtypeStruct(value.shape, value.dtype),
        compiler_params=pltpu.CompilerParams(vmem_limit_bytes=8 * MIB),
        name="hold",
    )(value)


def pack_kernel(place, energy, *refs):
    pieces, out = refs[:-1], refs[-1]
    scale = jnp.exp(0.5 * energy[...])
    for n, piece in enumerate(pieces):
        rows = pl.ds(pl.multiple_of(place[n] * 64, 64), 64)
        out[rows, :] = (piece[...].astype(F32) * scale).astype(BF16)


def pack(place, energy, pieces):
    whole = pl.BlockSpec(memory_space=pltpu.VMEM)
    return pl.pallas_call(
        pack_kernel,
        in_specs=[pl.BlockSpec(memory_space=pltpu.SMEM)] + [whole] * (1 + len(pieces)),
        out_specs=whole,
        out_shape=jax.ShapeDtypeStruct((256, energy.shape[1]), BF16),
        compiler_params=pltpu.CompilerParams(vmem_limit_bytes=8 * MIB),
        name="pack",
    )(place, energy, *pieces)


def rows_kernel(weight, rates, out):
    total = lax.dot_general(rates[...], weight[...], NT, preferred_element_type=F32)
    out[...] = total.astype(BF16)


def sum_rows(weight, rates):
    (depth, rows), columns = rates.shape, weight.shape[0]
    tile = 1376
    return pl.pallas_call(
        rows_kernel,
        grid=(pl.cdiv(depth, tile),),
        in_specs=[
            pl.BlockSpec((columns, rows), lambda s: (0, 0)),
            pl.BlockSpec((tile, rows), lambda s: (s, 0)),
        ],
        out_specs=pl.BlockSpec((tile, columns), lambda s: (s, 0)),
        out_shape=jax.ShapeDtypeStruct((depth, columns), BF16),
        compiler_params=pltpu.CompilerParams(
            dimension_semantics=("arbitrary",), vmem_limit_bytes=48 * MIB
        ),
        cost_estimate=pl.CostEstimate(
            flops=2 * rows * depth * columns,
            bytes_accessed=2 * depth * (rows + columns),
            transcendentals=0,
        ),
        name="sum_rows",
    )(weight, rates)


def columns_kernel(place, *refs):
    blocks, energy, pairs, out, total = refs[:8], refs[8], (refs[9:11], refs[11:13]), *refs[13:]
    depth, tile = energy.shape[1], 1024

    for start in range(0, depth, tile):
        part = slice(start, min(start + tile, depth))
        scale = jnp.exp(-0.5 * energy[:, part])
        basis = jnp.concatenate(
            [(block[:, part].astype(F32) * scale).astype(BF16) for block in blocks], axis=0
        )
        for k, (left, right) in enumerate(pairs):
            both = (left[part, :].astype(F32) + right[part, :].astype(F32)).astype(BF16)
            product = jnp.dot(basis, both, preferred_element_type=F32)
            half = slice(256 * k, 256 * k + 256)
            total[:, half] = product if start == 0 else total[:, half] + product

    left = lax.broadcasted_iota(jnp.int32, (8, 128), 1) < 64
    for n in range(16):
        for i in range(4):
            low = total[16 * n : 16 * n + 8, 128 * i : 128 * i + 128]
            high = total[16 * n + 8 : 16 * n + 16, 128 * i : 128 * i + 128]
            first = jnp.where(left, low, pltpu.roll(high, 64, 1))
            second = jnp.where(left, pltpu.roll(low, 64, 1), high)
            pair = jnp.concatenate([first, second], axis=0)
            to = place[n] * 64 + place[16 + i // 2] * 32 + 16 * (i % 2)
            out[pl.ds(pl.multiple_of(to, 16), 16), :] = pair.astype(BF16)


def sum_columns(place, blocks, energy, pairs):
    depth = energy.shape[1]
    whole = pl.BlockSpec(memory_space=pltpu.VMEM)
    return pl.pallas_call(
        columns_kernel,
        in_specs=[pl.BlockSpec(memory_space=pltpu.SMEM)] + [whole] * (len(blocks) + 5),
        out_specs=whole,
        out_shape=jax.ShapeDtypeStruct((1024, 128), BF16),
        scratch_shapes=[pltpu.VMEM((256, 512), F32)],
        compiler_params=pltpu.CompilerParams(vmem_limit_bytes=24 * MIB),
        cost_estimate=pl.CostEstimate(
            flops=2 * 256 * 512 * depth,
            bytes_accessed=4 * depth * 512 + 2 * 256 * depth,
            transcendentals=depth,
        ),
        name="sum_columns",
    )(place, *blocks, energy, *pairs[0], *pairs[1])


def finish_kernel(parts, out):
    total = jnp.sum(parts[...].astype(F32).reshape(128, 8, 128), axis=0)
    out[...] = jnp.concatenate([total[:, :64], total[:, 64:]], axis=0)


def finish(parts):
    return pl.pallas_call(
        finish_kernel,
        out_shape=jax.ShapeDtypeStruct((16, 64), F32),
        compiler_params=pltpu.CompilerParams(vmem_limit_bytes=8 * MIB),
        name="finish",
    )(parts).T


def shards(rates, trial, test, col_energy, row_energy):
    rates, trial, test = rates.T, trial.T, test.T
    xh, z, xl, y = (lax.axis_index(axis) for axis in PEERS)
    sign_y, sign_z = 1 - 2 * (y % 2), 1 - 2 * (z % 2)

    def hops(n):
        return swap(held[1 - n], "z"), swap(held[n - 1], "z", 1)

    held = {0: join(hold(trial), swap(trial, "xh"))}

    tests = {0: test, 1: swap(test, "y"), -1: swap(test, "y", 1), 2: cross(test, "y")}
    place = jnp.stack([(y + h * sign_y + 4) % 4 for h in tests]).astype(jnp.int32)
    place = after(place, held[0])
    weight = pack(place, row_energy[None, :], list(tests.values()))
    beside = swap(weight, "xl")

    held[1], held[-1] = together(*hops(1))
    near = sum_rows(after(weight, held[1]), rates)
    held[2], held[-2], near = together(*hops(2), near)
    far = sum_rows(after(beside, held[2]), rates)
    held[3], held[-3], far = together(*hops(3), far)
    near, far = ((part, swap(part, "core")) for part in (near, far))
    held[4] = swap(held[-3], "z")

    place = [((xh + k) % 2) * 8 + (z + h * sign_z + 8) % 8 for h in held for k in range(2)]
    place = jnp.stack([*place, xl, 1 - xl]).astype(jnp.int32)
    parts = sum_columns(place, list(held.values()), col_energy[None, :], (near, far))
    parts = lax.all_to_all(parts.reshape(128, 8, 128), PEERS, 0, 0)
    return finish(parts.reshape(1024, 128))


def solution(mesh):
    split = Mesh(mesh.devices.reshape(tuple(SIZES.values())), tuple(SIZES))
    placed = (P(ROW, COL), P(COL, ROW), P(ROW, COL), P(COL), P(ROW))
    return jax.shard_map(
        shards, mesh=split, in_specs=placed, out_specs=P(COL, ROW), check_vma=False
    )
```

```python
import jax
import jax.numpy as jnp
from jax import lax
from jax.experimental import pallas as pl
from jax.experimental.pallas import tpu as pltpu
from jax.sharding import Mesh
from jax.sharding import PartitionSpec as P

SIZES = {"xh": 2, "z": 8, "core": 2, "xl": 2, "y": 4}
ROW, COL = ("xh", "z", "core"), ("xl", "y")
PEERS = ("xh", "z", "xl", "y")
F32, BF16 = jnp.float32, jnp.bfloat16
NT = (((1,), (1,)), ((), ()))
MIB = 2**20
HOPS = (0, 1, -1, 2, -2, 3, -3, 4)


def swap(value, axis, side=0):
    n = SIZES[axis]
    pairs = [((i + side) % n, (i + 1 + side) % n) for i in range(0, n, 2)]
    return lax.ppermute(value, axis, pairs + [(b, a) for a, b in pairs])


def cross(value, axis):
    n = SIZES[axis]
    return lax.ppermute(value, axis, [(i, (i + n // 2) % n) for i in range(n)])


def together(*values):
    return lax.optimization_barrier(values)


def after(value, *others):
    return together(value, *others)[0]


def join_kernel(first, second, out):
    out[...] = jnp.concatenate([first[...], second[...]], axis=0)


def join(first, second):
    rows, columns = first.shape
    return pl.pallas_call(
        join_kernel,
        out_shape=jax.ShapeDtypeStruct((2 * rows, columns), first.dtype),
        compiler_params=pltpu.CompilerParams(vmem_limit_bytes=8 * MIB),
        name="join",
    )(first, second)


def hold_kernel(value, out):
    out[...] = value[...]


def hold(value):
    return pl.pallas_call(
        hold_kernel,
        out_shape=jax.ShapeDtypeStruct(value.shape, value.dtype),
        compiler_params=pltpu.CompilerParams(vmem_limit_bytes=8 * MIB),
        name="hold",
    )(value)


def pack_kernel(place, energy, *refs):
    pieces, out = refs[:-1], refs[-1]
    scale = jnp.exp(0.5 * energy[...])
    for n, piece in enumerate(pieces):
        rows = pl.ds(pl.multiple_of(place[n] * 64, 64), 64)
        out[rows, :] = (piece[...].astype(F32) * scale).astype(BF16)


def pack(place, energy, pieces):
    whole = pl.BlockSpec(memory_space=pltpu.VMEM)
    return pl.pallas_call(
        pack_kernel,
        in_specs=[pl.BlockSpec(memory_space=pltpu.SMEM)] + [whole] * (1 + len(pieces)),
        out_specs=whole,
        out_shape=jax.ShapeDtypeStruct((256, energy.shape[1]), BF16),
        compiler_params=pltpu.CompilerParams(vmem_limit_bytes=8 * MIB),
        name="pack",
    )(place, energy, *pieces)


def parts_of(depth, tile=1024):
    starts = range(0, depth - tile + 1, tile)
    return [pl.ds(n, tile if n + 2 * tile <= depth else depth - n) for n in starts]


def rows_of(weight, rates, part):
    total = lax.dot_general(rates[part, :], weight[...], NT, preferred_element_type=F32)
    return total.astype(BF16)


def rows_kernel(weight, rates, out, held, arrived):
    copies = [
        (part, pltpu.make_async_copy(rates.at[part, :], held.at[part, :], arrived.at[n]))
        for n, part in enumerate(parts_of(rates.shape[0]))
    ]
    for _, copy in copies:
        copy.start()
    for part, copy in copies:
        copy.wait()
        out[part, :] = rows_of(weight, held, part)


def sum_rows(weight, rates):
    (depth, rows), columns = rates.shape, weight.shape[0]
    whole = pl.BlockSpec(memory_space=pltpu.VMEM)
    return pl.pallas_call(
        rows_kernel,
        in_specs=[whole, pl.BlockSpec(memory_space=pl.ANY)],
        out_specs=whole,
        out_shape=jax.ShapeDtypeStruct((depth, columns), BF16),
        scratch_shapes=[
            pltpu.VMEM((depth, rows), BF16),
            pltpu.SemaphoreType.DMA((len(parts_of(depth)),)),
        ],
        compiler_params=pltpu.CompilerParams(vmem_limit_bytes=48 * MIB),
        cost_estimate=pl.CostEstimate(
            flops=2 * rows * depth * columns,
            bytes_accessed=2 * depth * (rows + columns),
            transcendentals=0,
        ),
        name="sum_rows",
    )(weight, rates)


def columns_kernel(place, *refs):
    blocks, energy, pairs, out, total = refs[:8], refs[8], (refs[9:11], refs[11:13]), *refs[13:]
    for n, part in enumerate(parts_of(energy.shape[1])):
        scale = jnp.exp(-0.5 * energy[:, part])
        basis = jnp.concatenate(
            [(block[:, part].astype(F32) * scale).astype(BF16) for block in blocks], axis=0
        )
        for k, (left, right) in enumerate(pairs):
            both = left[part, :] + right[part, :]
            product = jnp.dot(basis, both, preferred_element_type=F32)
            half = slice(256 * k, 256 * k + 256)
            total[:, half] = product if n == 0 else total[:, half] + product

    left = lax.broadcasted_iota(jnp.int32, (8, 128), 1) < 64
    for n in range(16):
        for i in range(4):
            low = total[16 * n : 16 * n + 8, 128 * i : 128 * i + 128]
            high = total[16 * n + 8 : 16 * n + 16, 128 * i : 128 * i + 128]
            first = jnp.where(left, low, pltpu.roll(high, 64, 1))
            second = jnp.where(left, pltpu.roll(low, 64, 1), high)
            pair = jnp.concatenate([first, second], axis=0)
            to = place[n] * 64 + place[16 + i // 2] * 32 + 16 * (i % 2)
            out[pl.ds(pl.multiple_of(to, 16), 16), :] = pair.astype(BF16)


def sum_columns(place, blocks, energy, pairs):
    depth = energy.shape[1]
    whole = pl.BlockSpec(memory_space=pltpu.VMEM)
    return pl.pallas_call(
        columns_kernel,
        in_specs=[pl.BlockSpec(memory_space=pltpu.SMEM)] + [whole] * (len(blocks) + 5),
        out_specs=whole,
        out_shape=jax.ShapeDtypeStruct((1024, 128), BF16),
        scratch_shapes=[pltpu.VMEM((256, 512), F32)],
        compiler_params=pltpu.CompilerParams(vmem_limit_bytes=24 * MIB),
        cost_estimate=pl.CostEstimate(
            flops=2 * 256 * 512 * depth,
            bytes_accessed=4 * depth * 512 + 2 * 256 * depth,
            transcendentals=depth,
        ),
        name="sum_columns",
    )(place, *blocks, energy, *pairs[0], *pairs[1])


def finish_kernel(parts, out):
    total = jnp.sum(parts[...].astype(F32).reshape(128, 8, 128), axis=0)
    out[...] = jnp.concatenate([total[:, :64], total[:, 64:]], axis=0)


def finish(parts):
    return pl.pallas_call(
        finish_kernel,
        out_shape=jax.ShapeDtypeStruct((16, 64), F32),
        compiler_params=pltpu.CompilerParams(vmem_limit_bytes=8 * MIB),
        name="finish",
    )(parts).T


def shards(rates, trial, test, col_energy, row_energy):
    rates, trial, test = rates.T, trial.T, test.T
    xh, z, xl, y = (lax.axis_index(axis) for axis in PEERS)
    sign_y, sign_z = 1 - 2 * (y % 2), 1 - 2 * (z % 2)

    def hops(n):
        return swap(held[1 - n], "z"), swap(held[n - 1], "z", 1)

    held = {0: join(hold(trial), swap(trial, "xh"))}

    tests = {0: test, 1: swap(test, "y"), -1: swap(test, "y", 1), 2: cross(test, "y")}
    place = jnp.stack([(y + h * sign_y + 4) % 4 for h in tests]).astype(jnp.int32)
    place = after(place, held[0])
    weight = pack(place, row_energy[None, :], list(tests.values()))
    beside = swap(weight, "xl")

    held[1], held[-1] = together(*hops(1))
    spots = [((xh + k) % 2) * 8 + (z + h * sign_z + 8) % 8 for h in HOPS for k in range(2)]
    spots = jnp.stack([*spots, xl, 1 - xl]).astype(jnp.int32)
    weight, spots, energy, _ = together(weight, spots, col_energy[None, :], held[1])
    near = sum_rows(weight, rates)
    held[2], held[-2], near = together(*hops(2), near)
    far = sum_rows(after(beside, held[2]), rates)
    held[3], held[-3], far = together(*hops(3), far)
    near, far = ((part, swap(part, "core")) for part in (near, far))
    held[4] = swap(held[-3], "z")

    parts = sum_columns(spots, list(held.values()), energy, (near, far))
    parts = lax.all_to_all(parts.reshape(128, 8, 128), PEERS, 0, 0)
    return finish(parts.reshape(1024, 128))


def solution(mesh):
    split = Mesh(mesh.devices.reshape(tuple(SIZES.values())), tuple(SIZES))
    placed = (P(ROW, COL), P(COL, ROW), P(ROW, COL), P(COL), P(ROW))
    return jax.shard_map(
        shards, mesh=split, in_specs=placed, out_specs=P(COL, ROW), check_vma=False
    )
```

```python
import functools

import jax
import jax.numpy as jnp
from jax import lax
from jax.experimental import pallas as pl
from jax.experimental.pallas import tpu as pltpu
from jax.sharding import Mesh
from jax.sharding import PartitionSpec as P

SIZES = {"xh": 2, "z": 8, "core": 2, "xl": 2, "y": 4}
ROW, COL = ("xh", "z", "core"), ("xl", "y")
PEERS = ("xh", "z", "xl", "y")
F32, BF16 = jnp.float32, jnp.bfloat16
NT = (((1,), (1,)), ((), ()))
MIB = 2**20
HOPS = (0, 1, -1, 2, -2, 3, -3)


def swap(value, axis, side=0):
    n = SIZES[axis]
    pairs = [((i + side) % n, (i + 1 + side) % n) for i in range(0, n, 2)]
    return lax.ppermute(value, axis, pairs + [(b, a) for a, b in pairs])


def cross(value, axis):
    n = SIZES[axis]
    return lax.ppermute(value, axis, [(i, (i + n // 2) % n) for i in range(n)])


def together(*values):
    return lax.optimization_barrier(values)


def after(value, *others):
    return together(value, *others)[0]


def join_kernel(first, second, out):
    out[...] = jnp.concatenate([first[...], second[...]], axis=0)


def join(first, second):
    rows, columns = first.shape
    return pl.pallas_call(
        join_kernel,
        out_shape=jax.ShapeDtypeStruct((2 * rows, columns), first.dtype),
        compiler_params=pltpu.CompilerParams(vmem_limit_bytes=8 * MIB),
        name="join",
    )(first, second)


def hold_kernel(value, out):
    out[...] = value[...]


def hold(value):
    return pl.pallas_call(
        hold_kernel,
        out_shape=jax.ShapeDtypeStruct(value.shape, value.dtype),
        compiler_params=pltpu.CompilerParams(vmem_limit_bytes=8 * MIB),
        name="hold",
    )(value)


def half_kernel(value, out, *, start):
    out[...] = value[start : start + out.shape[0], :]


def half(value, start):
    rows, columns = value.shape
    return pl.pallas_call(
        functools.partial(half_kernel, start=start),
        out_shape=jax.ShapeDtypeStruct((rows // 2, columns), value.dtype),
        compiler_params=pltpu.CompilerParams(vmem_limit_bytes=8 * MIB),
        name="half",
    )(value)


def pack_kernel(place, energy, *refs):
    pieces, out = refs[:-1], refs[-1]
    scale = jnp.exp(0.5 * energy[...])
    for n, piece in enumerate(pieces):
        rows = pl.ds(pl.multiple_of(place[n] * 64, 64), 64)
        out[rows, :] = (piece[...].astype(F32) * scale).astype(BF16)


def pack(place, energy, pieces):
    whole = pl.BlockSpec(memory_space=pltpu.VMEM)
    return pl.pallas_call(
        pack_kernel,
        in_specs=[pl.BlockSpec(memory_space=pltpu.SMEM)] + [whole] * (1 + len(pieces)),
        out_specs=whole,
        out_shape=jax.ShapeDtypeStruct((256, energy.shape[1]), BF16),
        compiler_params=pltpu.CompilerParams(vmem_limit_bytes=8 * MIB),
        name="pack",
    )(place, energy, *pieces)


def parts_of(depth, tile=1024):
    starts = range(0, depth - tile + 1, tile)
    return [pl.ds(n, tile if n + 2 * tile <= depth else depth - n) for n in starts]


def rows_kernel(weight, rates, out):
    total = lax.dot_general(rates[...], weight[...], NT, preferred_element_type=F32)
    out[...] = total.astype(BF16)


def sum_rows(weight, rates):
    (depth, rows), columns = rates.shape, weight.shape[0]
    whole = pl.BlockSpec(memory_space=pltpu.VMEM)
    return pl.pallas_call(
        rows_kernel,
        in_specs=[whole, whole],
        out_specs=whole,
        out_shape=jax.ShapeDtypeStruct((depth, columns), BF16),
        compiler_params=pltpu.CompilerParams(vmem_limit_bytes=16 * MIB),
        cost_estimate=pl.CostEstimate(
            flops=2 * rows * depth * columns,
            bytes_accessed=2 * depth * (rows + columns),
            transcendentals=0,
        ),
        name="sum_rows",
    )(weight, rates)


def columns_kernel(place, *refs):
    blocks, energy, pairs, out, total = refs[:9], refs[9], (refs[10:12], refs[12:14]), *refs[14:]
    for n, part in enumerate(parts_of(energy.shape[1])):
        scale = jnp.exp(-0.5 * energy[:, part])
        basis = jnp.concatenate(
            [(block[:, part].astype(F32) * scale).astype(BF16) for block in blocks], axis=0
        )
        for k, (left, right) in enumerate(pairs):
            both = left[part, :] + right[part, :]
            product = jnp.dot(basis, both, preferred_element_type=F32)
            half = slice(256 * k, 256 * k + 256)
            total[:, half] = product if n == 0 else total[:, half] + product

    left = lax.broadcasted_iota(jnp.int32, (8, 128), 1) < 64
    for n in range(16):
        for i in range(4):
            low = total[16 * n : 16 * n + 8, 128 * i : 128 * i + 128]
            high = total[16 * n + 8 : 16 * n + 16, 128 * i : 128 * i + 128]
            first = jnp.where(left, low, pltpu.roll(high, 64, 1))
            second = jnp.where(left, pltpu.roll(low, 64, 1), high)
            pair = jnp.concatenate([first, second], axis=0)
            to = place[n] * 64 + place[16 + i // 2] * 32 + 16 * (i % 2)
            out[pl.ds(pl.multiple_of(to, 16), 16), :] = pair.astype(BF16)


def sum_columns(place, blocks, energy, pairs):
    depth = energy.shape[1]
    whole = pl.BlockSpec(memory_space=pltpu.VMEM)
    return pl.pallas_call(
        columns_kernel,
        in_specs=[pl.BlockSpec(memory_space=pltpu.SMEM)] + [whole] * (len(blocks) + 5),
        out_specs=whole,
        out_shape=jax.ShapeDtypeStruct((1024, 128), BF16),
        scratch_shapes=[pltpu.VMEM((256, 512), F32)],
        compiler_params=pltpu.CompilerParams(vmem_limit_bytes=24 * MIB),
        cost_estimate=pl.CostEstimate(
            flops=2 * 256 * 512 * depth,
            bytes_accessed=4 * depth * 512 + 2 * 256 * depth,
            transcendentals=depth,
        ),
        name="sum_columns",
    )(place, *blocks, energy, *pairs[0], *pairs[1])


def finish_kernel(parts, out):
    total = jnp.sum(parts[...].astype(F32).reshape(128, 8, 128), axis=0)
    out[...] = jnp.concatenate([total[:, :64], total[:, 64:]], axis=0)


def finish(parts):
    return pl.pallas_call(
        finish_kernel,
        out_shape=jax.ShapeDtypeStruct((16, 64), F32),
        compiler_params=pltpu.CompilerParams(vmem_limit_bytes=8 * MIB),
        name="finish",
    )(parts).T


def shards(rates, trial, test, col_energy, row_energy):
    rates, trial, test = rates.T, trial.T, test.T
    xh, z, xl, y = (lax.axis_index(axis) for axis in PEERS)
    sign_y, sign_z = 1 - 2 * (y % 2), 1 - 2 * (z % 2)

    def hops(n):
        return swap(held[1 - n], "z"), swap(held[n - 1], "z", 1)

    held = {0: join(hold(trial), swap(trial, "xh"))}

    tests = {0: test, 1: swap(test, "y"), -1: swap(test, "y", 1), 2: cross(test, "y")}
    place = jnp.stack([(y + h * sign_y + 4) % 4 for h in tests]).astype(jnp.int32)
    place = after(place, held[0])
    weight = pack(place, row_energy[None, :], list(tests.values()))
    beside = swap(weight, "xl")

    held[1], held[-1] = together(*hops(1))
    spots = [((xh + k) % 2) * 8 + (z + h * sign_z + 8) % 8 for h in HOPS for k in range(2)]
    spots += [xh * 8 + (z + 4) % 8, (1 - xh) * 8 + (z + 4) % 8]
    spots = jnp.stack([*spots, xl, 1 - xl]).astype(jnp.int32)
    weight, spots, energy, _ = together(weight, spots, col_energy[None, :], held[1])
    near = sum_rows(weight, rates)
    held[2], held[-2], near = together(*hops(2), near)
    far = sum_rows(after(beside, held[2]), rates)
    held[3], held[-3], far = together(*hops(3), far)
    near, far = ((part, swap(part, "core")) for part in (near, far))
    held[4], held[-4] = swap(half(held[-3], 0), "z"), swap(half(held[3], 16), "z", 1)

    parts = sum_columns(spots, list(held.values()), energy, (near, far))
    parts = lax.all_to_all(parts.reshape(128, 8, 128), PEERS, 0, 0)
    return finish(parts.reshape(1024, 128))


def solution(mesh):
    split = Mesh(mesh.devices.reshape(tuple(SIZES.values())), tuple(SIZES))
    placed = (P(ROW, COL), P(COL, ROW), P(ROW, COL), P(COL), P(ROW))
    return jax.shard_map(
        shards, mesh=split, in_specs=placed, out_specs=P(COL, ROW), check_vma=False
    )
```

```python
import functools

import jax
import jax.numpy as jnp
from jax import lax
from jax.experimental import pallas as pl
from jax.experimental.pallas import tpu as pltpu
from jax.sharding import Mesh
from jax.sharding import PartitionSpec as P

SIZES = {"xh": 2, "z": 8, "core": 2, "xl": 2, "y": 4}
ROW, COL = ("xh", "z", "core"), ("xl", "y")
PEERS = ("xh", "z", "xl", "y")
F32, BF16 = jnp.float32, jnp.bfloat16
NT = (((1,), (1,)), ((), ()))
MIB = 2**20
HOPS = (0, 1, -1, 2, -2, 3, -3)


def swap(value, axis, side=0):
    n = SIZES[axis]
    pairs = [((i + side) % n, (i + 1 + side) % n) for i in range(0, n, 2)]
    return lax.ppermute(value, axis, pairs + [(b, a) for a, b in pairs])


def cross(value, axis):
    n = SIZES[axis]
    return lax.ppermute(value, axis, [(i, (i + n // 2) % n) for i in range(n)])


def together(*values):
    return lax.optimization_barrier(values)


def after(value, *others):
    return together(value, *others)[0]


def join_kernel(first, second, out):
    out[...] = jnp.concatenate([first[...], second[...]], axis=0)


def join(first, second):
    rows, columns = first.shape
    return pl.pallas_call(
        join_kernel,
        out_shape=jax.ShapeDtypeStruct((2 * rows, columns), first.dtype),
        compiler_params=pltpu.CompilerParams(vmem_limit_bytes=8 * MIB),
        name="join",
    )(first, second)


def hold_kernel(value, out):
    out[...] = value[...]


def hold(value):
    return pl.pallas_call(
        hold_kernel,
        out_shape=jax.ShapeDtypeStruct(value.shape, value.dtype),
        compiler_params=pltpu.CompilerParams(vmem_limit_bytes=8 * MIB),
        name="hold",
    )(value)


def half_kernel(value, out, *, start):
    out[...] = value[start : start + out.shape[0], :]


def half(value, start):
    rows, columns = value.shape
    return pl.pallas_call(
        functools.partial(half_kernel, start=start),
        out_shape=jax.ShapeDtypeStruct((rows // 2, columns), value.dtype),
        compiler_params=pltpu.CompilerParams(vmem_limit_bytes=8 * MIB),
        name="half",
    )(value)


def pack_kernel(place, energy, *refs):
    pieces, out = refs[:-1], refs[-1]
    scale = jnp.exp(0.5 * energy[...])
    for n, piece in enumerate(pieces):
        rows = pl.ds(pl.multiple_of(place[n] * 64, 64), 64)
        out[rows, :] = (piece[...].astype(F32) * scale).astype(BF16)


def pack(place, energy, pieces):
    whole = pl.BlockSpec(memory_space=pltpu.VMEM)
    return pl.pallas_call(
        pack_kernel,
        in_specs=[pl.BlockSpec(memory_space=pltpu.SMEM)] + [whole] * (1 + len(pieces)),
        out_specs=whole,
        out_shape=jax.ShapeDtypeStruct((256, energy.shape[1]), BF16),
        compiler_params=pltpu.CompilerParams(vmem_limit_bytes=8 * MIB),
        name="pack",
    )(place, energy, *pieces)


def parts_of(depth, tile=1024):
    starts = range(0, depth - tile + 1, tile)
    return [pl.ds(n, tile if n + 2 * tile <= depth else depth - n) for n in starts]


def rows_kernel(weight, rates, out):
    total = lax.dot_general(rates[...], weight[...], NT, preferred_element_type=F32)
    out[...] = total.astype(BF16)


def sum_rows(weight, rates):
    (depth, rows), columns = rates.shape, weight.shape[0]
    whole = pl.BlockSpec(memory_space=pltpu.VMEM)
    return pl.pallas_call(
        rows_kernel,
        in_specs=[whole, whole],
        out_specs=whole,
        out_shape=jax.ShapeDtypeStruct((depth, columns), BF16),
        compiler_params=pltpu.CompilerParams(vmem_limit_bytes=16 * MIB),
        cost_estimate=pl.CostEstimate(
            flops=2 * rows * depth * columns,
            bytes_accessed=2 * depth * (rows + columns),
            transcendentals=0,
        ),
        name="sum_rows",
    )(weight, rates)


def columns_kernel(*refs):
    blocks, energy, left, right, out, total = refs[:9], *refs[9:]
    for n, part in enumerate(parts_of(energy.shape[1])):
        scale = jnp.exp(-0.5 * energy[:, part])
        basis = jnp.concatenate(
            [(block[:, part].astype(F32) * scale).astype(BF16) for block in blocks], axis=0
        )
        product = jnp.dot(basis, left[part, :] + right[part, :], preferred_element_type=F32)
        total[...] = product if n == 0 else total[...] + product
    out[...] = total[...].astype(out.dtype)


def sum_columns(blocks, energy, pair, dtype):
    depth = energy.shape[1]
    whole = pl.BlockSpec(memory_space=pltpu.VMEM)
    return pl.pallas_call(
        columns_kernel,
        in_specs=[whole] * (len(blocks) + 3),
        out_specs=whole,
        out_shape=jax.ShapeDtypeStruct((256, 256), dtype),
        scratch_shapes=[pltpu.VMEM((256, 256), F32)],
        compiler_params=pltpu.CompilerParams(vmem_limit_bytes=16 * MIB),
        cost_estimate=pl.CostEstimate(
            flops=2 * 256 * 256 * depth,
            bytes_accessed=4 * depth * 256 + 2 * 256 * depth,
            transcendentals=depth,
        ),
        name="sum_columns",
    )(*blocks, energy, *pair)


def merge_kernel(place, near, far, out):
    left = lax.broadcasted_iota(jnp.int32, (8, 128), 1) < 64
    for n in range(16):
        both = near[16 * n : 16 * n + 16, :] + far[16 * n : 16 * n + 16, :].astype(F32)
        for i in range(2):
            low = both[:8, 128 * i : 128 * i + 128]
            high = both[8:, 128 * i : 128 * i + 128]
            first = jnp.where(left, low, pltpu.roll(high, 64, 1))
            second = jnp.where(left, pltpu.roll(low, 64, 1), high)
            pair = jnp.concatenate([first, second], axis=0)
            rows = pl.ds(pl.multiple_of(place[n] * 32 + 16 * i, 16), 16)
            out[rows, :] = pair.astype(BF16)


def merge(place, near, far):
    whole = pl.BlockSpec(memory_space=pltpu.VMEM)
    return pl.pallas_call(
        merge_kernel,
        in_specs=[pl.BlockSpec(memory_space=pltpu.SMEM), whole, whole],
        out_specs=whole,
        out_shape=jax.ShapeDtypeStruct((512, 128), BF16),
        compiler_params=pltpu.CompilerParams(vmem_limit_bytes=8 * MIB),
        name="merge",
    )(place, near, far)


def finish_kernel(parts, out):
    total = jnp.sum(parts[...].astype(F32).reshape(64, 8, 128), axis=0)
    out[...] = jnp.concatenate([total[:, :64], total[:, 64:]], axis=0)


def finish(parts):
    return pl.pallas_call(
        finish_kernel,
        out_shape=jax.ShapeDtypeStruct((16, 64), F32),
        compiler_params=pltpu.CompilerParams(vmem_limit_bytes=8 * MIB),
        name="finish",
    )(parts).T


def shards(rates, trial, test, col_energy, row_energy):
    rates, trial, test = rates.T, trial.T, test.T
    xh, z, xl, y = (lax.axis_index(axis) for axis in PEERS)
    sign_y, sign_z = 1 - 2 * (y % 2), 1 - 2 * (z % 2)

    def hops(n):
        return swap(held[1 - n], "z"), swap(held[n - 1], "z", 1)

    held = {0: join(hold(trial), swap(trial, "xh"))}

    tests = {0: test, 1: swap(test, "y"), -1: swap(test, "y", 1), 2: cross(test, "y")}
    place = jnp.stack([(y + h * sign_y + 4) % 4 for h in tests]).astype(jnp.int32)
    place = after(place, held[0])
    weight = pack(place, row_energy[None, :], list(tests.values()))
    beside = swap(weight, "xl")

    held[1], held[-1] = together(*hops(1))
    spots = [((xh + k) % 2) * 8 + (z + h * sign_z + 8) % 8 for h in HOPS for k in range(2)]
    spots += [xh * 8 + (z + 4) % 8, (1 - xh) * 8 + (z + 4) % 8]
    spots = jnp.stack(spots).astype(jnp.int32)
    weight, spots, energy, _ = together(weight, spots, col_energy[None, :], held[1])
    near = sum_rows(weight, rates)
    held[2], held[-2], near = together(*hops(2), near)
    far = sum_rows(after(beside, held[2]), rates)
    held[3], held[-3], far = together(*hops(3), far)
    near, far = ((part, swap(part, "core")) for part in (near, far))
    held[4], held[-4] = swap(half(held[-3], 0), "z"), swap(half(held[3], 16), "z", 1)

    blocks = list(held.values())
    far, near = together(far, near)
    far = swap(sum_columns(blocks, energy, far, BF16), "xl")
    near = sum_columns(blocks, energy, near, F32)
    parts = merge(spots, near, far).reshape(64, 8, 128)
    parts = lax.all_to_all(parts, ("xh", "z", "y"), 0, 0)
    return finish(parts.reshape(512, 128))


def solution(mesh):
    split = Mesh(mesh.devices.reshape(tuple(SIZES.values())), tuple(SIZES))
    placed = (P(ROW, COL), P(COL, ROW), P(ROW, COL), P(COL), P(ROW))
    return jax.shard_map(
        shards, mesh=split, in_specs=placed, out_specs=P(COL, ROW), check_vma=False
    )
```
